256 devices in a mesh: seg: 16 (over z, core), bond: 16 (over x, y).
Axes of the slice: x: 4, y: 4, z: 8, core: 2. Of those that a mesh axis runs over, the one named last changes fastest.
Arguments:
- left_env: bfloat16 [16, 1024, 6, 1024], P('seg', 'bond'), may hold values from -0.1875 to 0.1875
- prev_left: bfloat16 [16, 1024, 1024], P('seg'), may hold values from -0.25 to 1.25
- cur_site: bfloat16 [16, 1024, 4, 1024], P('seg', 'bond'), may hold values from -6 to 6
- prev_site: bfloat16 [16, 1024, 4, 1024], P('seg', None, None, 'bond'), may hold values from -6 to 6
- hamiltonian: bfloat16 [16, 6, 6, 4, 4], P('seg'), may hold values from -1.25 to 1.25
- right_env: bfloat16 [16, 1024, 6, 1024], P('seg', 'bond'), may hold values from -0.078125 to 0.078125
- prev_right: bfloat16 [16, 1024, 1024], P('seg'), may hold values from -0.25 to 1.25
Outputs:
- new_site: bfloat16 [16, 1024, 4, 1024], P('seg', 'bond')
- center: float32 [16, 1024, 1024], P('seg', 'bond')
The draws below stay inside these ranges and needn't reach their ends.
All inputs are finite; a program needn't handle non-finite values.
Results may differ from the reference program's by a relative error of at most 0.0054.
Values may be sent and summed in bfloat16 or wider, within the bound.
No kernel may reach another device: no remote copies, remote signals or barrier semaphores. Data moves between devices by JAX's collectives and lax.ppermute only.
A program may use at most 128 MiB of HBM per device.

```python
import math
import jax
import jax.numpy as jnp
from jax import lax

CHI = 1024
PHYS = 4
MPOB = 6
SEGMENTS = 16


def dominant_square(key):
    noise = jax.random.normal(key, (SEGMENTS, CHI, CHI), jnp.float32)
    noise = jnp.clip(noise * (0.5 / math.sqrt(CHI)), -0.25, 0.25)
    return noise + jnp.eye(CHI, dtype=jnp.float32)[None]


def draw_prev_left(key, part):
    return dominant_square(jax.random.fold_in(key, 11)).astype(jnp.bfloat16)


def draw_prev_right(key, part):
    return dominant_square(jax.random.fold_in(key, 23)).astype(jnp.bfloat16)


def draw_prev_site(key, part):
    first = jax.random.fold_in(key, 37)
    base = jax.random.normal(first, (SEGMENTS, CHI, PHYS, CHI), jnp.float32)
    return jnp.clip(base, -6.0, 6.0).astype(jnp.bfloat16)


def block_levels(rng, extent, cuts, low, top_value):
    level, own = 1.0, jax.random.fold_in(rng, 6)
    for position, parts in cuts:
        heights = jnp.exp(jax.random.uniform(jax.random.fold_in(own, position), (parts,), jnp.float32, low / len(cuts), top_value / len(cuts)))
        level = level * jnp.repeat(heights, extent[position] // parts).reshape([-1 if axis == position else 1 for axis in range(len(extent))])
    return level


def gaussian(stream_key, dims, deviation, most, split=(), kind=jnp.bfloat16):
    values = jax.random.normal(stream_key, dims, jnp.float32) * deviation
    if len(split) > 0:
        values = block_levels(stream_key, dims, split, -0.22, 0.18) * values
    return jnp.clip(values, min=-most, max=most).astype(kind)


def setup_inputs(seed: int = 0) -> dict:
    streams_of = jax.random.split(jax.random.key(seed), 8)
    return {
        "left_env": gaussian(streams_of[0], (SEGMENTS, CHI, MPOB, CHI), CHI ** -0.5, 0.1875, ((0, 16), (1, 16))),
        "prev_left": draw_prev_left(jax.random.fold_in(streams_of[7], 71), 0),
        "cur_site": gaussian(streams_of[2], (SEGMENTS, CHI, PHYS, CHI), 1.0, 6.0, ((0, 16), (1, 16))),
        "prev_site": draw_prev_site(jax.random.fold_in(streams_of[7], 71), 0),
        "hamiltonian": gaussian(streams_of[4], (SEGMENTS, MPOB, MPOB, PHYS, PHYS), (MPOB * PHYS) ** -0.5, 1.25, ((0, 16),)),
        "right_env": gaussian(streams_of[5], (SEGMENTS, CHI, MPOB, CHI), (MPOB * CHI) ** -0.5, 0.078125, ((0, 16), (1, 16))),
        "prev_right": draw_prev_right(jax.random.fold_in(streams_of[7], 71), 0),
    }


def segment_step(pieces):
    left_now, prev_now, current, previous, hamiltonian, right_block, prev_block = pieces
    projected = jnp.dot(left_now.reshape(CHI * MPOB, CHI).astype(jnp.float32), current.reshape(CHI, PHYS * CHI).astype(jnp.float32), preferred_element_type=jnp.float32).reshape(CHI, MPOB, PHYS, CHI)
    mixture = jnp.einsum('autc,uvst->asvc', projected, hamiltonian.astype(jnp.float32), precision=lax.Precision.HIGHEST).astype(jnp.bfloat16)
    right_flat = jnp.transpose(right_block, (1, 0, 2)).reshape(MPOB * CHI, CHI)
    applied = jnp.dot(mixture.reshape(CHI * PHYS, MPOB * CHI).astype(jnp.float32), right_flat.astype(jnp.float32), preferred_element_type=jnp.float32)
    partial_value = jnp.dot(prev_now.astype(jnp.float32), previous.reshape(CHI, PHYS * CHI).astype(jnp.float32), preferred_element_type=jnp.float32).astype(jnp.bfloat16)
    second = jnp.dot(partial_value.reshape(CHI * PHYS, CHI).astype(jnp.float32), prev_block.astype(jnp.float32), preferred_element_type=jnp.float32)
    target = 2.0 * applied - second
    correlation = jnp.dot(target.T.astype(jnp.float32), target.astype(jnp.float32), precision=lax.Precision.HIGHEST, preferred_element_type=jnp.float32)
    triangle = jnp.linalg.cholesky(correlation)
    solved = jax.scipy.linalg.solve_triangular(triangle, target.T, lower=True)
    norming = math.sqrt(CHI * PHYS)
    new_site = (solved.T * norming).astype(jnp.bfloat16).reshape(CHI, PHYS, CHI)
    center = triangle.T / norming
    return (new_site, center)

def reference(left_env, prev_left, cur_site, prev_site, hamiltonian, right_env, prev_right):
    left_now = jnp.roll(left_env, 1, axis=0)
    prev_now = jnp.roll(prev_left, 1, axis=0)
    new_site, center = lax.map(segment_step, (left_now, prev_now, cur_site, prev_site, hamiltonian, right_env, prev_right))
    return (new_site, center)
```

```python
import functools
import math

import jax
import jax.numpy as jnp
from jax import lax
from jax.experimental import pallas as pl
from jax.experimental.pallas import tpu as pltpu
from jax.sharding import Mesh
from jax.sharding import PartitionSpec as P

PHYS = 4
MPOB = 6
CHI = 1024
BLOCK = 128
MICRO = 16
STEPS = CHI // BLOCK
PACKED = STEPS * (STEPS + 1) // 2 * BLOCK
NORMING = math.sqrt(CHI * PHYS)
BOND = ("bx", "by")


def block_row(i, j):
    return (i * STEPS - i * (i - 1) // 2 + j - i) * BLOCK


def exact_dot(a, b, ca, cb):
    return lax.dot_general(
        a,
        b,
        (((ca,), (cb,)), ((), ())),
        precision=lax.Precision.HIGHEST,
        preferred_element_type=jnp.float32,
    )


def correlation_kernel(target_ref, packed_ref):
    for i in range(STEPS):
        rows = exact_dot(target_ref[:, i * BLOCK : (i + 1) * BLOCK], target_ref[:, i * BLOCK :], 0, 0)
        for j in range(i, STEPS):
            o = (j - i) * BLOCK
            packed_ref[block_row(i, j) : block_row(i, j) + BLOCK, :] = rows[:, o : o + BLOCK]


def factor_block(work_ref, done_ref):
    def step(b, carry):
        base = pl.multiple_of(b * MICRO, MICRO)
        block = work_ref[pl.ds(base, MICRO), :]
        left = pltpu.roll(block[:, :BLOCK], BLOCK - base, 1)
        rows = [jnp.broadcast_to(block[t : t + 1], (8, 2 * BLOCK)) for t in range(MICRO)]
        s = [[None] * MICRO for _ in range(MICRO)]
        for r in range(MICRO):
            row = jnp.broadcast_to(left[r : r + 1], (8, BLOCK))
            for t in range(r, MICRO):
                s[r][t] = jnp.broadcast_to(row[:, t : t + 1], (8, BLOCK))
        for r in range(MICRO):
            inverse = 1.0 / s[r][r]
            scale = lax.rsqrt(s[r][r])
            factors = {t: s[r][t] * inverse for t in range(r + 1, MICRO)}
            for t in range(r + 1, MICRO):
                for q in range(t, MICRO):
                    s[t][q] = s[t][q] - factors[t] * s[r][q]
            for t in range(r + 1, MICRO):
                rows[t] = rows[t] - jnp.concatenate([factors[t], factors[t]], 1) * rows[r]
            rows[r] = rows[r] * jnp.concatenate([scale, scale], 1)
        u = jnp.concatenate([rows[t][0:1] for t in range(MICRO)], 0)
        done_ref[pl.ds(base, MICRO), :] = u
        work_ref[...] = work_ref[...] - exact_dot(u[:, :BLOCK], u, 0, 0)
        return carry

    lax.fori_loop(0, BLOCK // MICRO, step, 0)


def fit_kernel(index_ref, packed_ref, target_ref, site_ref, center_ref, s_ref, t_ref, work_ref, done_ref):
    row = lax.broadcasted_iota(jnp.int32, (BLOCK, BLOCK), 0)
    column = lax.broadcasted_iota(jnp.int32, (BLOCK, BLOCK), 1)
    for i in range(STEPS):
        for j in range(STEPS):
            if j >= i:
                block = packed_ref[block_row(i, j) : block_row(i, j) + BLOCK, :]
            else:
                block = jnp.zeros((BLOCK, BLOCK), jnp.float32)
            s_ref[i * BLOCK : (i + 1) * BLOCK, j * BLOCK : (j + 1) * BLOCK] = block
    t_ref[...] = target_ref[...]
    for k in range(STEPS):
        a, b = k * BLOCK, (k + 1) * BLOCK
        work_ref[:, :BLOCK] = s_ref[a:b, a:b]
        work_ref[:, BLOCK:] = (row == column).astype(jnp.float32)
        factor_block(work_ref, done_ref)
        s_ref[a:b, a:b] = jnp.where(row <= column, done_ref[:, :BLOCK], 0.0)
        inverse = done_ref[:, BLOCK:]
        solved = exact_dot(t_ref[:, a:b], inverse, 1, 1)
        site_ref[:, a:b] = (solved * NORMING).astype(jnp.bfloat16)
        if b < CHI:
            panel = exact_dot(inverse, s_ref[a:b, b:], 1, 0)
            s_ref[a:b, b:] = panel
            t_ref[:, b:] = t_ref[:, b:] - exact_dot(solved, panel, 1, 0)
            for i in range(k + 1, STEPS):
                o = i * BLOCK - b
                rows = slice(i * BLOCK, (i + 1) * BLOCK)
                s_ref[rows, i * BLOCK :] = s_ref[rows, i * BLOCK :] - exact_dot(
                    panel[:, o : o + BLOCK], panel[:, o:], 0, 0
                )
    own = center_ref.shape[0]
    center_ref[...] = s_ref[pl.ds(pl.multiple_of(index_ref[0] * own, own), own), :] * (1.0 / NORMING)


VMEM = pl.BlockSpec(memory_space=pltpu.VMEM)


def correlate(target):
    return pl.pallas_call(
        correlation_kernel,
        out_shape=jax.ShapeDtypeStruct((PACKED, BLOCK), jnp.float32),
        in_specs=[VMEM],
        out_specs=VMEM,
        compiler_params=pltpu.CompilerParams(vmem_limit_bytes=24 * 2**20),
    )(target)


def fit(index, packed, target):
    rows = target.shape[0]
    return pl.pallas_call(
        fit_kernel,
        out_shape=(
            jax.ShapeDtypeStruct((rows, CHI), jnp.bfloat16),
            jax.ShapeDtypeStruct((rows // PHYS, CHI), jnp.float32),
        ),
        in_specs=[pl.BlockSpec(memory_space=pltpu.SMEM), VMEM, VMEM],
        out_specs=(VMEM, VMEM),
        scratch_shapes=[
            pltpu.VMEM((CHI, CHI), jnp.float32),
            pltpu.VMEM((rows, CHI), jnp.float32),
            pltpu.VMEM((BLOCK, 2 * BLOCK), jnp.float32),
            pltpu.VMEM((BLOCK, 2 * BLOCK), jnp.float32),
        ],
        compiler_params=pltpu.CompilerParams(vmem_limit_bytes=40 * 2**20),
    )(index, packed, target)


def shifted(block, axis, distance):
    count = lax.axis_size(axis)
    return lax.ppermute(block, axis, [((i - distance) % count, i) for i in range(count)])


def placed(block, axis):
    count = lax.axis_size(axis)
    me = lax.axis_index(axis)
    whole = jnp.zeros((count,) + block.shape, block.dtype)
    for d in range(count):
        piece = shifted(block, axis, d) if d else block
        whole = lax.dynamic_update_index_in_dim(whole, piece, lax.rem(me + count - d, count), 0)
    return whole


def shards(left_env, prev_left, cur_site, prev_site, hamiltonian, right_env, prev_right):
    own = left_env.shape[1]
    group = 4 * own
    left_own = shifted(left_env[0].reshape(own * MPOB, CHI), "seg", 1)
    prev_now = shifted(prev_left[0], "seg", 1)
    coupling = hamiltonian[0].astype(jnp.float32)

    split = jnp.transpose(cur_site[0].reshape(own, PHYS, 4, group), (2, 0, 1, 3))
    split = lax.all_to_all(split.reshape(4, own, PHYS * group), "bx", 0, 0, tiled=True)
    current = jnp.transpose(placed(split, "by"), (1, 0, 2, 3)).reshape(CHI, PHYS * group)
    right = placed(right_env[0].reshape(own, MPOB * CHI), "by").reshape(group, MPOB, CHI)
    left_now = jnp.stack([left_own] + [shifted(left_own, "bx", d) for d in (1, 2, 3)])

    partial_value = jnp.einsum(
        "ab,bsc->asc", prev_now, prev_site[0], preferred_element_type=jnp.float32
    ).astype(jnp.bfloat16)
    partial_value = lax.all_to_all(
        partial_value.reshape(16, own * PHYS, own), BOND, 0, 0, tiled=True
    )
    partial_value = jnp.transpose(partial_value, (1, 0, 2)).reshape(own * PHYS, CHI)
    second = jnp.dot(partial_value, prev_right[0], preferred_element_type=jnp.float32)

    projected = jnp.dot(
        left_now.reshape(group * MPOB, CHI), current, preferred_element_type=jnp.float32
    ).reshape(group, MPOB, PHYS, group)
    mixture = jnp.einsum(
        "autc,uvst->asvc", projected, coupling, precision=lax.Precision.HIGHEST
    ).astype(jnp.bfloat16)
    applied = jnp.einsum("asvc,cvy->asy", mixture, right, preferred_element_type=jnp.float32)
    applied = applied.reshape(4, own * PHYS, CHI)
    total = applied[0]
    for d in (1, 3, 2):
        total = total + shifted(applied[d].astype(jnp.bfloat16), "bx", -d).astype(jnp.float32)
    target = 2.0 * total - second

    packed = correlate(target)
    share = PACKED // 16
    packed = lax.all_to_all(packed.reshape(16, share, BLOCK), BOND, 0, 0, tiled=True)
    packed = jnp.broadcast_to(packed.sum(0)[None], (16, share, BLOCK))
    packed = lax.all_to_all(packed, BOND, 0, 0, tiled=True).reshape(PACKED, BLOCK)
    new_site, center = fit(lax.axis_index(BOND).reshape(1), packed, target)
    return (new_site.reshape(1, own, PHYS, CHI), center[None])


def solution(mesh):
    segments, bonds = mesh.devices.shape
    side = math.isqrt(bonds)
    grid = Mesh(mesh.devices.reshape(segments, side, side), ("seg", "bx", "by"))
    return jax.shard_map(
        shards,
        mesh=grid,
        in_specs=(
            P("seg", BOND, None, None),
            P("seg", None, None),
            P("seg", BOND, None, None),
            P("seg", None, None, BOND),
            P("seg", None, None, None, None),
            P("seg", BOND, None, None),
            P("seg", None, None),
        ),
        out_specs=(P("seg", BOND, None, None), P("seg", BOND, None)),
        check_vma=False,
    )
```

```python
import functools
import math

import jax
import jax.numpy as jnp
from jax import lax
from jax.experimental import pallas as pl
from jax.experimental.pallas import tpu as pltpu
from jax.sharding import Mesh
from jax.sharding import PartitionSpec as P

PHYS = 4
MPOB = 6
CHI = 1024
BLOCK = 128
MICRO = 32
LANES = 8
STEPS = CHI // BLOCK
SHARE = STEPS * (STEPS + 1) // 2 * BLOCK // 8
NORMING = math.sqrt(CHI * PHYS)
BOND = ("bx", "by")


def exact_dot(a, b, ca, cb):
    return lax.dot_general(
        a,
        b,
        (((ca,), (cb,)), ((), ())),
        precision=lax.Precision.HIGHEST,
        preferred_element_type=jnp.float32,
    )


def wide_dot(a, b):
    return jnp.dot(a, b, preferred_element_type=jnp.float32)


def mix_kernel(place_ref, coupling_ref, *refs):
    left_refs, sites_ref, out_refs = refs[0:4], refs[4], refs[5:9]
    site_ref, projected_ref = refs[9:]
    own = sites_ref.shape[2]
    width = site_ref.shape[1] // PHYS
    for y in range(4):
        for d in range(4):
            start = (place_ref[0, d] * 4 + y) * own
            site_ref[pl.ds(pl.multiple_of(start, own), own), :] = sites_ref[y, d]
    for d in range(4):
        for t in range(PHYS):
            columns = slice(t * width, (t + 1) * width)
            projected_ref[d % 2, :, columns] = wide_dot(left_refs[d][...], site_ref[:, columns])
        for g in range(own // LANES):
            pieces = [
                projected_ref[
                    d % 2, u * own + g * LANES : u * own + (g + 1) * LANES, t * width : (t + 1) * width
                ]
                for t in range(PHYS)
                for u in range(MPOB)
            ]
            value = jnp.concatenate(pieces, 0)
            high = value.astype(jnp.bfloat16)
            low = (value - high.astype(jnp.float32)).astype(jnp.bfloat16)
            mixed = wide_dot(coupling_ref[...], high) + wide_dot(coupling_ref[...], low)
            mixed = mixed.astype(jnp.bfloat16)
            count = LANES * PHYS
            for v in range(MPOB):
                out_refs[d][g * count : (g + 1) * count, v * width : (v + 1) * width] = mixed[
                    v * count : (v + 1) * count
                ]


def gather_right(place_ref, piece_refs, previous_ref, right_ref):
    own = piece_refs[0].shape[0] // MPOB
    group = 4 * own
    for d in range(4):
        start = place_ref[1, d] * own
        for v in range(MPOB):
            rows = pl.ds(pl.multiple_of(v * group + start, own), own)
            right_ref[rows, :] = piece_refs[d][v * own : (v + 1) * own, :]
        rows = slice(MPOB * group + d * own, MPOB * group + (d + 1) * own)
        right_ref[rows, :] = previous_ref[pl.ds(pl.multiple_of(start, own), own), :]


def apply_kernel(distances, place_ref, *refs):
    count = len(distances)
    piece_refs, previous_ref, partial_ref = refs[0:4], refs[4], refs[5]
    mixed_refs, out_refs, right_ref = refs[6 : 6 + count], refs[6 + count : -1], refs[-1]
    gather_right(place_ref, piece_refs, previous_ref, right_ref)
    depth = mixed_refs[0].shape[1]
    for d, mixed_ref, out_ref in zip(distances, mixed_refs, out_refs):
        for n in range(4):
            columns = slice(n * CHI // 4, (n + 1) * CHI // 4)
            value = wide_dot(mixed_ref[...], right_ref[:depth, columns])
            value = value + wide_dot(partial_ref[place_ref[0, d]], right_ref[depth:, columns])
            out_ref[:, columns] = value.astype(out_ref.dtype)


def correlation_kernel(place_ref, own_ref, *refs):
    arrived_refs, target_ref, share_refs, packed_ref = refs[0:3], refs[3], refs[4:12], refs[12]
    total = own_ref[...]
    for ref in arrived_refs:
        total = total + ref[...].astype(jnp.float32)
    target_ref[...] = 2.0 * total
    o = 0
    for i in range(STEPS):
        rows = exact_dot(target_ref[:, i * BLOCK : (i + 1) * BLOCK], target_ref[:, i * BLOCK :], 0, 0)
        for j in range(STEPS - i):
            packed_ref[o : o + BLOCK, :] = rows[:, j * BLOCK : (j + 1) * BLOCK]
            o += BLOCK
    for half in range(2):
        for d in range(4):
            start = (half * 4 + place_ref[half, (4 - d) % 4]) * SHARE
            share_refs[half * 4 + d][...] = packed_ref[pl.ds(pl.multiple_of(start, 8), SHARE), :]


def factor_rows(block, base):
    groups = MICRO // 8
    iota = lax.broadcasted_iota(jnp.int32, (8, BLOCK), 0)
    c = {}
    for t in range(MICRO):
        for g in range(t // 8, groups):
            c[t, g] = jnp.broadcast_to(block[8 * g : 8 * g + 8, base + t : base + t + 1], (8, BLOCK))
    rows = [
        [block[8 * g : 8 * g + 8, h * BLOCK : (h + 1) * BLOCK] for h in range(2)]
        for g in range(groups)
    ]
    scale = [jnp.ones((8, BLOCK), jnp.float32) for _ in range(groups)]
    for r in range(MICRO):
        gr, ro = r // 8, r % 8
        pivot = jnp.broadcast_to(c[r, gr][ro : ro + 1], (8, BLOCK))
        inverse = 1.0 / pivot
        m = {g: c[r, g] * inverse for g in range(gr, groups)}
        m[gr] = jnp.where(iota > ro, m[gr], 0.0)
        for t in range(r + 1, MICRO):
            entry = jnp.broadcast_to(c[r, t // 8][t % 8 : t % 8 + 1], (8, BLOCK))
            for g in range(t // 8, groups):
                c[t, g] = c[t, g] - m[g] * entry
        for h in range(2):
            row = jnp.broadcast_to(rows[gr][h][ro : ro + 1], (8, BLOCK))
            for g in range(gr, groups):
                rows[g][h] = rows[g][h] - m[g] * row
        scale[gr] = jnp.where(iota == ro, lax.rsqrt(pivot), scale[gr])
    return jnp.concatenate(
        [jnp.concatenate([rows[g][h] * scale[g] for h in range(2)], 1) for g in range(groups)], 0
    )


def fit_kernel(index_ref, place_ref, *refs):
    share_refs, target_ref, site_ref, center_ref = refs[0:8], refs[8], refs[9], refs[10]
    packed_ref, s_ref, t_ref, work_ref, done_ref, semaphores = refs[11:]
    copies = [pltpu.make_async_copy(target_ref, t_ref, semaphores.at[8])]
    for half in range(2):
        for d in range(4):
            n = half * 4 + d
            start = (half * 4 + place_ref[half, d]) * SHARE
            rows = packed_ref.at[pl.ds(pl.multiple_of(start, 8), SHARE), :]
            copies.append(pltpu.make_async_copy(share_refs[n], rows, semaphores.at[n]))
    for copy in copies:
        copy.start()
    for copy in copies:
        copy.wait()
    steps = size = STEPS
    row = lax.broadcasted_iota(jnp.int32, (BLOCK, BLOCK), 0)
    column = lax.broadcasted_iota(jnp.int32, (BLOCK, BLOCK), 1)
    o = 0
    for i in range(size):
        rows = slice(i * BLOCK, (i + 1) * BLOCK)
        for j in range(size):
            columns = slice(j * BLOCK, (j + 1) * BLOCK)
            block = jnp.zeros((BLOCK, BLOCK), jnp.float32)
            if j >= i:
                block = packed_ref[o : o + BLOCK, :]
                o += BLOCK
            s_ref[rows, columns] = block
    pending = []
    for k in range(steps):
        a, b = k * BLOCK, (k + 1) * BLOCK
        work, done = work_ref.at[k % 2], done_ref.at[k % 2]
        work[:, :BLOCK] = s_ref[a:b, a:b]
        work[:, BLOCK:] = (row == column).astype(jnp.float32)
        count = BLOCK // MICRO
        share = -(-len(pending) // count)
        for q in range(count):
            base = q * MICRO
            end = base + MICRO
            u = factor_rows(work[base:end, :], base)
            done[base:end, :] = u
            if end < BLOCK:
                factors = u[:, :BLOCK].T
                work[end:, :] = work[end:, :] - exact_dot(factors[end:], u, 1, 0)
            for update in pending[q * share : (q + 1) * share]:
                update()
        s_ref[a:b, a:b] = jnp.where(row <= column, done[:, :BLOCK], 0.0)
        inverse = done[:, BLOCK:]
        panel = None
        pending = []
        if k + 1 < size:
            panel = exact_dot(inverse, s_ref[a:b, b:], 1, 0)
            s_ref[a:b, b:] = panel

            def update_rows(i, panel=panel, b=b):
                o = i * BLOCK - b
                rows = slice(i * BLOCK, (i + 1) * BLOCK)
                s_ref[rows, i * BLOCK :] = s_ref[rows, i * BLOCK :] - exact_dot(
                    panel[:, o : o + BLOCK], panel[:, o:], 0, 0
                )

            update_rows(k + 1)
            pending = [functools.partial(update_rows, i) for i in range(k + 2, size)]

        def solve(a=a, b=b, inverse=inverse, panel=panel):
            solved = exact_dot(t_ref[:, a:b], inverse, 1, 1)
            site_ref[:, a:b] = (solved * NORMING).astype(jnp.bfloat16)
            if panel is not None:
                t_ref[:, b:] = t_ref[:, b:] - exact_dot(solved, panel, 1, 0)

        pending.append(solve)
        if k + 1 == steps:
            for update in pending:
                update()
    own = center_ref.shape[0]
    start = pl.multiple_of(index_ref[0] * own, own)
    center_ref[...] = s_ref[pl.ds(start, own), :] * (1.0 / NORMING)


VMEM = pl.BlockSpec(memory_space=pltpu.VMEM)
SMEM = pl.BlockSpec(memory_space=pltpu.SMEM)


def array(shape, dtype):
    return jax.ShapeDtypeStruct(shape, dtype)


def settings(mebibytes):
    return pltpu.CompilerParams(vmem_limit_bytes=mebibytes * 2**20)


def cost(flops, bytes_accessed):
    return pl.CostEstimate(flops=flops, bytes_accessed=bytes_accessed, transcendentals=0)


def mix(place, coupling, left, site):
    own = site.shape[2]
    group = 4 * own
    shape = array((own * PHYS, MPOB * group), jnp.bfloat16)
    return pl.pallas_call(
        mix_kernel,
        out_shape=(shape,) * 4,
        in_specs=[SMEM] + [VMEM] * 6,
        out_specs=(VMEM,) * 4,
        scratch_shapes=[
            pltpu.VMEM((CHI, PHYS * group), jnp.bfloat16),
            pltpu.VMEM((2, own * MPOB, PHYS * group), jnp.float32),
        ],
        compiler_params=settings(32),
        cost_estimate=cost(6 * 10**9, 9 * 10**6),
    )(place, coupling, *left, site)


def apply(distances, place, right, previous, partial_value, mixed, dtype):
    rows = mixed[0].shape[0]
    depth = 4 * (right[0].shape[0] + right[0].shape[0] // MPOB)
    count = len(distances)
    return pl.pallas_call(
        functools.partial(apply_kernel, distances),
        out_shape=(array((rows, CHI), dtype),) * count,
        in_specs=[SMEM] + [VMEM] * (6 + count),
        out_specs=(VMEM,) * count,
        scratch_shapes=[pltpu.VMEM((depth, CHI), jnp.bfloat16)],
        compiler_params=settings(32),
        cost_estimate=cost(2 * 10**9 * count, 6 * 10**6),
    )(place, *right, previous, partial_value, *mixed)


def correlate(place, own, arrived):
    return pl.pallas_call(
        correlation_kernel,
        out_shape=(array(own.shape, jnp.float32),) + (array((SHARE, BLOCK), jnp.float32),) * 8,
        in_specs=[SMEM] + [VMEM] * 4,
        out_specs=(VMEM,) * 9,
        scratch_shapes=[pltpu.VMEM((8 * SHARE, BLOCK), jnp.float32)],
        compiler_params=settings(24),
        cost_estimate=cost(3 * 10**9, 6 * 10**6),
    )(place, own, *arrived)


def fit(index, place, shares, target):
    rows = target.shape[0]
    return pl.pallas_call(
        fit_kernel,
        out_shape=(array((rows, CHI), jnp.bfloat16), array((rows // PHYS, CHI), jnp.float32)),
        in_specs=[SMEM] * 2 + [pl.BlockSpec(memory_space=pl.ANY)] * 9,
        out_specs=(VMEM,) * 2,
        scratch_shapes=[
            pltpu.VMEM((8 * SHARE, BLOCK), jnp.float32),
            pltpu.VMEM((CHI, CHI), jnp.float32),
            pltpu.VMEM((rows, CHI), jnp.float32),
            pltpu.VMEM((2, BLOCK, 2 * BLOCK), jnp.float32),
            pltpu.VMEM((2, BLOCK, 2 * BLOCK), jnp.float32),
            pltpu.SemaphoreType.DMA((9,)),
        ],
        compiler_params=settings(32),
        cost_estimate=cost(40 * 10**9, 8 * 10**6),
    )(index, place, *shares, target)


def shifted(block, axis, distance):
    count = lax.axis_size(axis)
    return lax.ppermute(block, axis, [((i - distance) % count, i) for i in range(count)])


def around(block, axis):
    return [block] + [shifted(block, axis, d) for d in (1, 2, 3)]


def scattered(blocks, axis):
    me = lax.axis_index(axis)
    out = []
    for d in range(4):
        block = lax.dynamic_index_in_dim(blocks, lax.rem(me + d, 4), 0, keepdims=False)
        out.append(shifted(block, axis, d) if d else block)
    return out


def summed(blocks):
    return (blocks[0] + blocks[1]) + (blocks[2] + blocks[3])


def shards(left_env, prev_left, cur_site, prev_site, hamiltonian, right_env, prev_right):
    own = left_env.shape[1]
    group = 4 * own
    left_own = jnp.transpose(left_env[0], (1, 0, 2)).reshape(MPOB * own, CHI)
    left_own = shifted(left_own, "seg", 1)
    x, y = lax.axis_index("bx"), lax.axis_index("by")
    place = jnp.stack([jnp.stack([lax.rem(i + 4 - d, 4) for d in range(4)]) for i in (x, y)])
    same = jnp.eye(LANES, dtype=jnp.bfloat16)
    coupling = jnp.transpose(hamiltonian[0], (1, 2, 3, 0))
    coupling = coupling[:, None, :, :, :, None] * same[None, :, None, None, None, :]
    coupling = coupling.reshape(MPOB * LANES * PHYS, PHYS * MPOB * LANES)

    split = jnp.transpose(cur_site[0].reshape(own, PHYS, 4, group), (2, 0, 1, 3))
    split = jnp.stack(scattered(split.reshape(4, own, PHYS * group), "bx"))
    right = jnp.transpose(right_env[0], (1, 0, 2)).reshape(MPOB * own, CHI)
    ahead, behind = shifted(right, "by", 1), shifted(right, "by", 3)
    prev_now, right, left_own, split, ahead, behind = lax.optimization_barrier(
        (prev_left[0], right, left_own, split, ahead, behind)
    )
    right = [right, ahead, shifted(right, "by", 2), behind]
    prev_now = shifted(prev_now, "seg", 1)
    site = lax.all_gather(split, "by", axis=0)
    left = around(left_own, "bx")

    partial_value = jnp.einsum(
        "ab,bsc->asc", prev_now, prev_site[0], preferred_element_type=jnp.float32
    )
    partial_value = (-0.5 * partial_value).astype(jnp.bfloat16)
    partial_value = jnp.transpose(partial_value.reshape(4, 4, own * PHYS, own), (1, 0, 2, 3))
    partial_value = jnp.concatenate(scattered(partial_value, "by"), 2)
    previous = lax.dynamic_slice_in_dim(prev_right[0], x * group, group, 0)

    mixed = mix(place, coupling, left, site)
    shared = (place, right, previous, partial_value)
    (far,) = apply((2,), *shared, mixed[2:3], jnp.bfloat16)
    near = apply((1, 3), *shared, mixed[1::2], jnp.bfloat16)
    (target,) = apply((0,), *shared, mixed[:1], jnp.float32)
    arrived = [shifted(v, "bx", -d) for v, d in ((far, 2), (near[0], 1), (near[1], 3))]
    target, *shares = correlate(place, target, arrived)

    halves = []
    for half, (axis, other) in enumerate((("bx", "by"), ("by", "bx"))):
        mine = shares[half * 4 : half * 4 + 4]
        mine = summed([mine[0]] + [shifted(mine[d], axis, d) for d in (1, 2, 3)])
        mine = summed(around(mine, other))
        halves += around(mine, axis)
    new_site, center = fit(lax.axis_index(BOND).reshape(1), place, halves, target)
    return (new_site.reshape(1, own, PHYS, CHI), center[None])


def solution(mesh):
    segments, bonds = mesh.devices.shape
    side = math.isqrt(bonds)
    grid = Mesh(mesh.devices.reshape(segments, side, side), ("seg", "bx", "by"))
    return jax.shard_map(
        shards,
        mesh=grid,
        in_specs=(
            P("seg", BOND, None, None),
            P("seg", None, None),
            P("seg", BOND, None, None),
            P("seg", None, None, BOND),
            P("seg", None, None, None, None),
            P("seg", BOND, None, None),
            P("seg", None, None),
        ),
        out_specs=(P("seg", BOND, None, None), P("seg", BOND, None)),
        check_vma=False,
    )
```

```python
import functools
import math

import jax
import jax.numpy as jnp
from jax import lax
from jax.experimental import pallas as pl
from jax.experimental.pallas import tpu as pltpu
from jax.sharding import Mesh
from jax.sharding import PartitionSpec as P

PHYS = 4
MPOB = 6
CHI = 1024
BLOCK = 128
MICRO = 32
LANES = 8
STEPS = CHI // BLOCK
SHARE = STEPS * (STEPS + 1) // 2 * BLOCK // 8
NORMING = math.sqrt(CHI * PHYS)
BOND = ("bx", "by")


def exact_dot(a, b, ca, cb):
    return lax.dot_general(
        a,
        b,
        (((ca,), (cb,)), ((), ())),
        precision=lax.Precision.HIGHEST,
        preferred_element_type=jnp.float32,
    )


def wide_dot(a, b):
    return jnp.dot(a, b, preferred_element_type=jnp.float32)


def mix_kernel(place_ref, coupling_ref, *refs):
    left_refs, sites_ref, out_refs = refs[0:4], refs[4], refs[5:9]
    site_ref, projected_ref = refs[9:]
    own = sites_ref.shape[2]
    width = site_ref.shape[1] // PHYS
    for y in range(4):
        for d in range(4):
            start = (place_ref[0, d] * 4 + y) * own
            site_ref[pl.ds(pl.multiple_of(start, own), own), :] = sites_ref[y, d]
    for d in range(4):
        for t in range(PHYS):
            columns = slice(t * width, (t + 1) * width)
            projected_ref[d % 2, :, columns] = wide_dot(left_refs[d][...], site_ref[:, columns])
        for g in range(own // LANES):
            pieces = [
                projected_ref[
                    d % 2, u * own + g * LANES : u * own + (g + 1) * LANES, t * width : (t + 1) * width
                ]
                for t in range(PHYS)
                for u in range(MPOB)
            ]
            value = jnp.concatenate(pieces, 0)
            high = value.astype(jnp.bfloat16)
            low = (value - high.astype(jnp.float32)).astype(jnp.bfloat16)
            mixed = wide_dot(coupling_ref[...], high) + wide_dot(coupling_ref[...], low)
            mixed = mixed.astype(jnp.bfloat16)
            count = LANES * PHYS
            for v in range(MPOB):
                out_refs[d][g * count : (g + 1) * count, v * width : (v + 1) * width] = mixed[
                    v * count : (v + 1) * count
                ]


def gather_right(place_ref, piece_refs, previous_ref, right_ref):
    own = piece_refs[0].shape[0] // MPOB
    group = 4 * own
    for d in range(4):
        start = place_ref[1, d] * own
        for v in range(MPOB):
            rows = pl.ds(pl.multiple_of(v * group + start, own), own)
            right_ref[rows, :] = piece_refs[d][v * own : (v + 1) * own, :]
        rows = slice(MPOB * group + d * own, MPOB * group + (d + 1) * own)
        right_ref[rows, :] = previous_ref[pl.ds(pl.multiple_of(start, own), own), :]


def apply_kernel(distances, place_ref, *refs):
    count = len(distances)
    piece_refs, previous_ref, partial_refs = refs[0:4], refs[4], refs[5:9]
    mixed_refs, out_refs, right_ref = refs[9 : 9 + count], refs[9 + count : -1], refs[-1]
    gather_right(place_ref, piece_refs, previous_ref, right_ref)
    depth = mixed_refs[0].shape[1]
    for d, mixed_ref, out_ref in zip(distances, mixed_refs, out_refs):
        partial_value = jnp.concatenate([ref[place_ref[0, d]] for ref in partial_refs], 1)
        for n in range(4):
            columns = slice(n * CHI // 4, (n + 1) * CHI // 4)
            value = wide_dot(mixed_ref[...], right_ref[:depth, columns])
            value = value + wide_dot(partial_value, right_ref[depth:, columns])
            out_ref[:, columns] = value.astype(out_ref.dtype)


def correlation_kernel(place_ref, own_ref, *refs):
    arrived_refs, target_ref, share_refs, packed_ref = refs[0:3], refs[3], refs[4:12], refs[12]
    total = own_ref[...]
    for ref in arrived_refs:
        total = total + ref[...].astype(jnp.float32)
    target_ref[...] = 2.0 * total
    o = 0
    for i in range(STEPS):
        rows = exact_dot(target_ref[:, i * BLOCK : (i + 1) * BLOCK], target_ref[:, i * BLOCK :], 0, 0)
        for j in range(STEPS - i):
            packed_ref[o : o + BLOCK, :] = rows[:, j * BLOCK : (j + 1) * BLOCK]
            o += BLOCK
    for half in range(2):
        for d in range(4):
            start = (half * 4 + place_ref[half, (4 - d) % 4]) * SHARE
            share_refs[half * 4 + d][...] = packed_ref[pl.ds(pl.multiple_of(start, 8), SHARE), :]


def factor_rows(block, base):
    groups = MICRO // 8
    iota = lax.broadcasted_iota(jnp.int32, (8, BLOCK), 0)
    c = {}
    for t in range(MICRO):
        for g in range(t // 8, groups):
            c[t, g] = jnp.broadcast_to(block[8 * g : 8 * g + 8, base + t : base + t + 1], (8, BLOCK))
    rows = [
        [block[8 * g : 8 * g + 8, h * BLOCK : (h + 1) * BLOCK] for h in range(2)]
        for g in range(groups)
    ]
    scale = [jnp.ones((8, BLOCK), jnp.float32) for _ in range(groups)]
    for r in range(MICRO):
        gr, ro = r // 8, r % 8
        pivot = jnp.broadcast_to(c[r, gr][ro : ro + 1], (8, BLOCK))
        inverse = 1.0 / pivot
        m = {g: c[r, g] * inverse for g in range(gr, groups)}
        m[gr] = jnp.where(iota > ro, m[gr], 0.0)
        for t in range(r + 1, MICRO):
            entry = jnp.broadcast_to(c[r, t // 8][t % 8 : t % 8 + 1], (8, BLOCK))
            for g in range(t // 8, groups):
                c[t, g] = c[t, g] - m[g] * entry
        for h in range(2):
            row = jnp.broadcast_to(rows[gr][h][ro : ro + 1], (8, BLOCK))
            for g in range(gr, groups):
                rows[g][h] = rows[g][h] - m[g] * row
        scale[gr] = jnp.where(iota == ro, lax.rsqrt(pivot), scale[gr])
    return jnp.concatenate(
        [jnp.concatenate([rows[g][h] * scale[g] for h in range(2)], 1) for g in range(groups)], 0
    )


def fit_kernel(index_ref, place_ref, *refs):
    share_refs, target_ref, site_ref, center_ref = refs[0:8], refs[8], refs[9], refs[10]
    packed_ref, s_ref, t_ref, work_ref, done_ref, semaphores = refs[11:]
    copies = [pltpu.make_async_copy(target_ref, t_ref, semaphores.at[8])]
    for half in range(2):
        for d in range(4):
            n = half * 4 + d
            start = (half * 4 + place_ref[half, d]) * SHARE
            rows = packed_ref.at[pl.ds(pl.multiple_of(start, 8), SHARE), :]
            copies.append(pltpu.make_async_copy(share_refs[n], rows, semaphores.at[n]))
    for copy in copies:
        copy.start()
    for copy in copies:
        copy.wait()
    steps = size = STEPS
    row = lax.broadcasted_iota(jnp.int32, (BLOCK, BLOCK), 0)
    column = lax.broadcasted_iota(jnp.int32, (BLOCK, BLOCK), 1)
    o = 0
    for i in range(size):
        rows = slice(i * BLOCK, (i + 1) * BLOCK)
        for j in range(size):
            columns = slice(j * BLOCK, (j + 1) * BLOCK)
            block = jnp.zeros((BLOCK, BLOCK), jnp.float32)
            if j >= i:
                block = packed_ref[o : o + BLOCK, :]
                o += BLOCK
            s_ref[rows, columns] = block
    pending = []
    for k in range(steps):
        a, b = k * BLOCK, (k + 1) * BLOCK
        work, done = work_ref.at[k % 2], done_ref.at[k % 2]
        work[:, :BLOCK] = s_ref[a:b, a:b]
        work[:, BLOCK:] = (row == column).astype(jnp.float32)
        count = BLOCK // MICRO
        share = -(-len(pending) // count)
        for q in range(count):
            base = q * MICRO
            end = base + MICRO
            u = factor_rows(work[base:end, :], base)
            done[base:end, :] = u
            if end < BLOCK:
                factors = u[:, :BLOCK].T
                work[end:, :] = work[end:, :] - exact_dot(factors[end:], u, 1, 0)
            for update in pending[q * share : (q + 1) * share]:
                update()
        s_ref[a:b, a:b] = jnp.where(row <= column, done[:, :BLOCK], 0.0)
        inverse = done[:, BLOCK:]
        panel = None
        pending = []
        if k + 1 < size:
            panel = exact_dot(inverse, s_ref[a:b, b:], 1, 0)
            s_ref[a:b, b:] = panel

            def update_rows(i, panel=panel, b=b):
                o = i * BLOCK - b
                rows = slice(i * BLOCK, (i + 1) * BLOCK)
                s_ref[rows, i * BLOCK :] = s_ref[rows, i * BLOCK :] - exact_dot(
                    panel[:, o : o + BLOCK], panel[:, o:], 0, 0
                )

            update_rows(k + 1)
            pending = [functools.partial(update_rows, i) for i in range(k + 2, size)]

        def solve(a=a, b=b, inverse=inverse, panel=panel):
            solved = exact_dot(t_ref[:, a:b], inverse, 1, 1)
            site_ref[:, a:b] = (solved * NORMING).astype(jnp.bfloat16)
            if panel is not None:
                t_ref[:, b:] = t_ref[:, b:] - exact_dot(solved, panel, 1, 0)

        pending.append(solve)
        if k + 1 == steps:
            for update in pending:
                update()
    own = center_ref.shape[0]
    start = pl.multiple_of(index_ref[0] * own, own)
    center_ref[...] = s_ref[pl.ds(start, own), :] * (1.0 / NORMING)


VMEM = pl.BlockSpec(memory_space=pltpu.VMEM)
SMEM = pl.BlockSpec(memory_space=pltpu.SMEM)


def array(shape, dtype):
    return jax.ShapeDtypeStruct(shape, dtype)


def settings(mebibytes):
    return pltpu.CompilerParams(vmem_limit_bytes=mebibytes * 2**20)


def cost(flops, bytes_accessed):
    return pl.CostEstimate(flops=flops, bytes_accessed=bytes_accessed, transcendentals=0)


def mix(place, coupling, left, site):
    own = site.shape[2]
    group = 4 * own
    shape = array((own * PHYS, MPOB * group), jnp.bfloat16)
    return pl.pallas_call(
        mix_kernel,
        out_shape=(shape,) * 4,
        in_specs=[SMEM] + [VMEM] * 6,
        out_specs=(VMEM,) * 4,
        scratch_shapes=[
            pltpu.VMEM((CHI, PHYS * group), jnp.bfloat16),
            pltpu.VMEM((2, own * MPOB, PHYS * group), jnp.float32),
        ],
        compiler_params=settings(24),
        cost_estimate=cost(6 * 10**9, 9 * 10**6),
    )(place, coupling, *left, site)


def apply(distances, place, right, previous, partial_value, mixed, dtype):
    rows = mixed[0].shape[0]
    depth = 4 * (right[0].shape[0] + right[0].shape[0] // MPOB)
    count = len(distances)
    return pl.pallas_call(
        functools.partial(apply_kernel, distances),
        out_shape=(array((rows, CHI), dtype),) * count,
        in_specs=[SMEM] + [VMEM] * (9 + count),
        out_specs=(VMEM,) * count,
        scratch_shapes=[pltpu.VMEM((depth, CHI), jnp.bfloat16)],
        compiler_params=settings(18),
        cost_estimate=cost(2 * 10**9 * count, 6 * 10**6),
    )(place, *right, previous, *partial_value, *mixed)


def correlate(place, own, arrived):
    return pl.pallas_call(
        correlation_kernel,
        out_shape=(array(own.shape, jnp.float32),) + (array((SHARE, BLOCK), jnp.float32),) * 8,
        in_specs=[SMEM] + [VMEM] * 4,
        out_specs=(VMEM,) * 9,
        scratch_shapes=[pltpu.VMEM((8 * SHARE, BLOCK), jnp.float32)],
        compiler_params=settings(16),
        cost_estimate=cost(3 * 10**9, 6 * 10**6),
    )(place, own, *arrived)


def fit(index, place, shares, target):
    rows = target.shape[0]
    return pl.pallas_call(
        fit_kernel,
        out_shape=(array((rows, CHI), jnp.bfloat16), array((rows // PHYS, CHI), jnp.float32)),
        in_specs=[SMEM] * 2 + [pl.BlockSpec(memory_space=pltpu.HBM)] * 9,
        out_specs=(VMEM,) * 2,
        scratch_shapes=[
            pltpu.VMEM((8 * SHARE, BLOCK), jnp.float32),
            pltpu.VMEM((CHI, CHI), jnp.float32),
            pltpu.VMEM((rows, CHI), jnp.float32),
            pltpu.VMEM((2, BLOCK, 2 * BLOCK), jnp.float32),
            pltpu.VMEM((2, BLOCK, 2 * BLOCK), jnp.float32),
            pltpu.SemaphoreType.DMA((9,)),
        ],
        compiler_params=settings(20),
        cost_estimate=cost(40 * 10**9, 8 * 10**6),
    )(index, place, *shares, target)


def shifted(block, axis, distance):
    count = lax.axis_size(axis)
    return lax.ppermute(block, axis, [((i - distance) % count, i) for i in range(count)])


def around(block, axis):
    return [block] + [shifted(block, axis, d) for d in (1, 2, 3)]


def scattered(blocks, axis):
    me = lax.axis_index(axis)
    out = []
    for d in range(4):
        block = lax.dynamic_index_in_dim(blocks, lax.rem(me + d, 4), 0, keepdims=False)
        out.append(shifted(block, axis, d) if d else block)
    return out


def summed(blocks):
    return (blocks[0] + blocks[1]) + (blocks[2] + blocks[3])


def shards(left_env, prev_left, cur_site, prev_site, hamiltonian, right_env, prev_right):
    own = left_env.shape[1]
    group = 4 * own
    left_own = jnp.transpose(left_env[0], (1, 0, 2)).reshape(MPOB * own, CHI)
    left_own = shifted(left_own, "seg", 1)
    x, y = lax.axis_index("bx"), lax.axis_index("by")
    place = jnp.stack([jnp.stack([lax.rem(i + 4 - d, 4) for d in range(4)]) for i in (x, y)])
    split = jnp.transpose(cur_site[0].reshape(own, PHYS, 4, group), (2, 0, 1, 3))
    split = jnp.stack(scattered(split.reshape(4, own, PHYS * group), "bx"))
    right = jnp.transpose(right_env[0], (1, 0, 2)).reshape(MPOB * own, CHI)
    ahead, behind = shifted(right, "by", 1), shifted(right, "by", 3)
    prev_now, right, left_own, split, ahead, behind = lax.optimization_barrier(
        (prev_left[0], right, left_own, split, ahead, behind)
    )
    right = [right, ahead, shifted(right, "by", 2), behind]
    prev_now = shifted(prev_now, "seg", 1)
    prev_now, hamiltonian = lax.optimization_barrier((prev_now, hamiltonian))
    same = jnp.eye(LANES, dtype=jnp.bfloat16)
    coupling = jnp.transpose(hamiltonian[0], (1, 2, 3, 0))
    coupling = coupling[:, None, :, :, :, None] * same[None, :, None, None, None, :]
    coupling = coupling.reshape(MPOB * LANES * PHYS, PHYS * MPOB * LANES)
    site = lax.all_gather(split, "by", axis=0)
    left = around(left_own, "bx")

    partial_value = jnp.einsum(
        "ab,bsc->asc", prev_now, prev_site[0], preferred_element_type=jnp.float32
    )
    partial_value = (-0.5 * partial_value).astype(jnp.bfloat16)
    partial_value = jnp.transpose(partial_value.reshape(4, 4, own * PHYS, own), (1, 0, 2, 3))
    partial_value, *_ = lax.optimization_barrier((partial_value, right[2], left[1], left[3]))
    partial_value = scattered(partial_value, "by")
    previous = lax.dynamic_slice_in_dim(prev_right[0], x * group, group, 0)

    mixed = mix(place, coupling, left, site)
    partial_value, mixed = lax.optimization_barrier((partial_value, mixed))
    shared = (place, right, previous, partial_value)
    (far,) = apply((2,), *shared, mixed[2:3], jnp.bfloat16)
    far, mixed = lax.optimization_barrier((far, mixed))
    near = apply((1, 3), *shared, mixed[1::2], jnp.bfloat16)
    (target,) = apply((0,), *shared, mixed[:1], jnp.float32)
    arrived = [shifted(v, "bx", -d) for v, d in ((far, 2), (near[0], 1), (near[1], 3))]
    target, *shares = correlate(place, target, arrived)

    halves = []
    for half, (axis, other) in enumerate((("bx", "by"), ("by", "bx"))):
        mine = shares[half * 4 : half * 4 + 4]
        mine = summed([mine[0]] + [shifted(mine[d], axis, d) for d in (1, 2, 3)])
        mine = summed(around(mine, other))
        halves += around(mine, axis)
    new_site, center = fit(lax.axis_index(BOND).reshape(1), place, halves, target)
    return (new_site.reshape(1, own, PHYS, CHI), center[None])


def solution(mesh):
    segments, bonds = mesh.devices.shape
    side = math.isqrt(bonds)
    grid = Mesh(mesh.devices.reshape(segments, side, side), ("seg", "bx", "by"))
    return jax.shard_map(
        shards,
        mesh=grid,
        in_specs=(
            P("seg", BOND, None, None),
            P("seg", None, None),
            P("seg", BOND, None, None),
            P("seg", None, None, BOND),
            P("seg", None, None, None, None),
            P("seg", BOND, None, None),
            P("seg", None, None),
        ),
        out_specs=(P("seg", BOND, None, None), P("seg", BOND, None)),
        check_vma=False,
    )
```

```python
import functools
import math

import jax
import jax.numpy as jnp
from jax import lax
from jax.experimental import pallas as pl
from jax.experimental.pallas import tpu as pltpu
from jax.sharding import Mesh
from jax.sharding import PartitionSpec as P

PHYS = 4
MPOB = 6
CHI = 1024
BLOCK = 128
MICRO = 32
LANES = 8
STEPS = CHI // BLOCK
SHARE = STEPS * (STEPS + 1) // 2 * BLOCK // 8
NORMING = math.sqrt(CHI * PHYS)
BOND = ("bx", "by")


def exact_dot(a, b, ca, cb):
    return lax.dot_general(
        a,
        b,
        (((ca,), (cb,)), ((), ())),
        precision=lax.Precision.HIGHEST,
        preferred_element_type=jnp.float32,
    )


def wide_dot(a, b):
    return jnp.dot(a, b, preferred_element_type=jnp.float32)


def mix_kernel(place_ref, coupling_ref, *refs):
    left_refs, sites_ref, out_refs = refs[0:4], refs[4], refs[5:9]
    site_ref, projected_ref = refs[9:]
    own = sites_ref.shape[2]
    width = site_ref.shape[1] // PHYS
    for y in range(4):
        for d in range(4):
            start = (place_ref[0, d] * 4 + y) * own
            site_ref[pl.ds(pl.multiple_of(start, own), own), :] = sites_ref[y, d]
    for d in range(4):
        for t in range(PHYS):
            columns = slice(t * width, (t + 1) * width)
            projected_ref[d % 2, :, columns] = wide_dot(left_refs[d][...], site_ref[:, columns])
        for g in range(own // LANES):
            pieces = [
                projected_ref[
                    d % 2, u * own + g * LANES : u * own + (g + 1) * LANES, t * width : (t + 1) * width
                ]
                for t in range(PHYS)
                for u in range(MPOB)
            ]
            value = jnp.concatenate(pieces, 0)
            high = value.astype(jnp.bfloat16)
            low = (value - high.astype(jnp.float32)).astype(jnp.bfloat16)
            mixed = wide_dot(coupling_ref[...], high) + wide_dot(coupling_ref[...], low)
            mixed = mixed.astype(jnp.bfloat16)
            count = LANES * PHYS
            for v in range(MPOB):
                out_refs[d][g * count : (g + 1) * count, v * width : (v + 1) * width] = mixed[
                    v * count : (v + 1) * count
                ]


def gather_right(place_ref, piece_refs, previous_ref, right_ref):
    own = piece_refs[0].shape[0] // MPOB
    group = 4 * own
    for d in range(4):
        start = place_ref[1, d] * own
        for v in range(MPOB):
            rows = pl.ds(pl.multiple_of(v * group + start, own), own)
            right_ref[rows, :] = piece_refs[d][v * own : (v + 1) * own, :]
        rows = slice(MPOB * group + d * own, MPOB * group + (d + 1) * own)
        right_ref[rows, :] = previous_ref[pl.ds(pl.multiple_of(start, own), own), :]


def apply_kernel(distances, place_ref, *refs):
    count = len(distances)
    piece_refs, previous_ref, partial_refs = refs[0:4], refs[4], refs[5:9]
    mixed_refs, out_refs, right_ref = refs[9 : 9 + count], refs[9 + count : -1], refs[-1]
    gather_right(place_ref, piece_refs, previous_ref, right_ref)
    depth = mixed_refs[0].shape[1]
    for d, mixed_ref, out_ref in zip(distances, mixed_refs, out_refs):
        partial_value = jnp.concatenate([ref[place_ref[0, d]] for ref in partial_refs], 1)
        for n in range(4):
            columns = slice(n * CHI // 4, (n + 1) * CHI // 4)
            value = wide_dot(mixed_ref[...], right_ref[:depth, columns])
            value = value + wide_dot(partial_value, right_ref[depth:, columns])
            out_ref[:, columns] = value.astype(out_ref.dtype)


def correlation_kernel(place_ref, own_ref, *refs):
    arrived_refs, target_ref, share_refs, packed_ref = refs[0:3], refs[3], refs[4:12], refs[12]
    total = own_ref[...]
    for ref in arrived_refs:
        total = total + ref[...].astype(jnp.float32)
    target_ref[...] = 2.0 * total
    o = 0
    for i in range(STEPS):
        rows = exact_dot(target_ref[:, i * BLOCK : (i + 1) * BLOCK], target_ref[:, i * BLOCK :], 0, 0)
        for j in range(STEPS - i):
            packed_ref[o : o + BLOCK, :] = rows[:, j * BLOCK : (j + 1) * BLOCK]
            o += BLOCK
    for half in range(2):
        for d in range(4):
            start = (half * 4 + place_ref[half, (4 - d) % 4]) * SHARE
            share_refs[half * 4 + d][...] = packed_ref[pl.ds(pl.multiple_of(start, 8), SHARE), :]


def factor_rows(block, base):
    groups = MICRO // 8
    iota = lax.broadcasted_iota(jnp.int32, (8, BLOCK), 0)
    c = {}
    for t in range(MICRO):
        for g in range(t // 8, groups):
            c[t, g] = jnp.broadcast_to(block[8 * g : 8 * g + 8, base + t : base + t + 1], (8, BLOCK))
    rows = [
        [block[8 * g : 8 * g + 8, h * BLOCK : (h + 1) * BLOCK] for h in range(2)]
        for g in range(groups)
    ]
    scale = [jnp.ones((8, BLOCK), jnp.float32) for _ in range(groups)]
    for r in range(MICRO):
        gr, ro = r // 8, r % 8
        pivot = jnp.broadcast_to(c[r, gr][ro : ro + 1], (8, BLOCK))
        inverse = 1.0 / pivot
        below = {g: c[r, g] for g in range(gr, groups)}
        below[gr] = jnp.where(iota > ro, below[gr], 0.0)
        m = {g: below[g] * inverse for g in below}
        for t in range(r + 1, MICRO):
            entry = jnp.broadcast_to(c[r, t // 8][t % 8 : t % 8 + 1], (8, BLOCK))
            for g in range(t // 8, groups):
                c[t, g] = c[t, g] - m[g] * entry
        for h in range(2):
            row = jnp.broadcast_to(rows[gr][h][ro : ro + 1], (8, BLOCK))
            for g in range(gr, groups):
                rows[g][h] = rows[g][h] - m[g] * row
        scale[gr] = jnp.where(iota == ro, lax.rsqrt(pivot), scale[gr])
    return jnp.concatenate(
        [jnp.concatenate([rows[g][h] * scale[g] for h in range(2)], 1) for g in range(groups)], 0
    )


def fit_kernel(index_ref, place_ref, *refs):
    share_refs, target_ref, site_ref, center_ref = refs[0:8], refs[8], refs[9], refs[10]
    packed_ref, s_ref, t_ref, work_ref, done_ref, semaphores = refs[11:]
    copies = [pltpu.make_async_copy(target_ref, t_ref, semaphores.at[8])]
    for half in range(2):
        for d in range(4):
            n = half * 4 + d
            start = (half * 4 + place_ref[half, d]) * SHARE
            rows = packed_ref.at[pl.ds(pl.multiple_of(start, 8), SHARE), :]
            copies.append(pltpu.make_async_copy(share_refs[n], rows, semaphores.at[n]))
    for copy in copies:
        copy.start()
    for copy in copies:
        copy.wait()
    steps = size = STEPS
    row = lax.broadcasted_iota(jnp.int32, (BLOCK, BLOCK), 0)
    column = lax.broadcasted_iota(jnp.int32, (BLOCK, BLOCK), 1)
    o = 0
    for i in range(size):
        rows = slice(i * BLOCK, (i + 1) * BLOCK)
        for j in range(size):
            columns = slice(j * BLOCK, (j + 1) * BLOCK)
            block = jnp.zeros((BLOCK, BLOCK), jnp.float32)
            if j >= i:
                block = packed_ref[o : o + BLOCK, :]
                o += BLOCK
            s_ref[rows, columns] = block
    pending = []
    for k in range(steps):
        a, b = k * BLOCK, (k + 1) * BLOCK
        work, done = work_ref.at[k % 2], done_ref.at[k % 2]
        work[:, :BLOCK] = s_ref[a:b, a:b]
        work[:, BLOCK:] = (row == column).astype(jnp.float32)
        count = BLOCK // MICRO
        share = -(-len(pending) // count)
        for q in range(count):
            base = q * MICRO
            end = base + MICRO
            u = factor_rows(work[base:end, :], base)
            done[base:end, :] = u
            if end < BLOCK:
                factors = u[:, :BLOCK].T
                work[end:, :] = work[end:, :] - exact_dot(factors[end:], u, 1, 0)
            for update in pending[q * share : (q + 1) * share]:
                update()
        s_ref[a:b, a:b] = jnp.where(row <= column, done[:, :BLOCK], 0.0)
        inverse = done[:, BLOCK:]
        panel = None
        pending = []
        if k + 1 < size:
            panel = exact_dot(inverse, s_ref[a:b, b:], 1, 0)
            s_ref[a:b, b:] = panel

            def update_rows(i, panel=panel, b=b):
                o = i * BLOCK - b
                rows = slice(i * BLOCK, (i + 1) * BLOCK)
                s_ref[rows, i * BLOCK :] = s_ref[rows, i * BLOCK :] - exact_dot(
                    panel[:, o : o + BLOCK], panel[:, o:], 0, 0
                )

            update_rows(k + 1)
            pending = [functools.partial(update_rows, i) for i in range(k + 2, size)]

        def solve(a=a, b=b, inverse=inverse, panel=panel):
            solved = exact_dot(t_ref[:, a:b], inverse, 1, 1)
            site_ref[:, a:b] = (solved * NORMING).astype(jnp.bfloat16)
            if panel is not None:
                t_ref[:, b:] = t_ref[:, b:] - exact_dot(solved, panel, 1, 0)

        pending.append(solve)
        if k + 1 == steps:
            for update in pending:
                update()
    own = center_ref.shape[0]
    start = pl.multiple_of(index_ref[0] * own, own)
    center_ref[...] = s_ref[pl.ds(start, own), :] * (1.0 / NORMING)


VMEM = pl.BlockSpec(memory_space=pltpu.VMEM)
SMEM = pl.BlockSpec(memory_space=pltpu.SMEM)


def array(shape, dtype):
    return jax.ShapeDtypeStruct(shape, dtype)


def settings(mebibytes):
    return pltpu.CompilerParams(vmem_limit_bytes=mebibytes * 2**20)


def cost(flops, bytes_accessed):
    return pl.CostEstimate(flops=flops, bytes_accessed=bytes_accessed, transcendentals=0)


def mix(place, coupling, left, site):
    own = site.shape[2]
    group = 4 * own
    shape = array((own * PHYS, MPOB * group), jnp.bfloat16)
    return pl.pallas_call(
        mix_kernel,
        out_shape=(shape,) * 4,
        in_specs=[SMEM] + [VMEM] * 6,
        out_specs=(VMEM,) * 4,
        scratch_shapes=[
            pltpu.VMEM((CHI, PHYS * group), jnp.bfloat16),
            pltpu.VMEM((2, own * MPOB, PHYS * group), jnp.float32),
        ],
        compiler_params=settings(24),
        cost_estimate=cost(6 * 10**9, 9 * 10**6),
    )(place, coupling, *left, site)


def apply(distances, place, right, previous, partial_value, mixed, dtype):
    rows = mixed[0].shape[0]
    depth = 4 * (right[0].shape[0] + right[0].shape[0] // MPOB)
    count = len(distances)
    return pl.pallas_call(
        functools.partial(apply_kernel, distances),
        out_shape=(array((rows, CHI), dtype),) * count,
        in_specs=[SMEM] + [VMEM] * (9 + count),
        out_specs=(VMEM,) * count,
        scratch_shapes=[pltpu.VMEM((depth, CHI), jnp.bfloat16)],
        compiler_params=settings(18),
        cost_estimate=cost(2 * 10**9 * count, 6 * 10**6),
    )(place, *right, previous, *partial_value, *mixed)


def correlate(place, own, arrived):
    return pl.pallas_call(
        correlation_kernel,
        out_shape=(array(own.shape, jnp.float32),) + (array((SHARE, BLOCK), jnp.float32),) * 8,
        in_specs=[SMEM] + [VMEM] * 4,
        out_specs=(VMEM,) * 9,
        scratch_shapes=[pltpu.VMEM((8 * SHARE, BLOCK), jnp.float32)],
        compiler_params=settings(16),
        cost_estimate=cost(3 * 10**9, 6 * 10**6),
    )(place, own, *arrived)


def fit(index, place, shares, target):
    rows = target.shape[0]
    return pl.pallas_call(
        fit_kernel,
        out_shape=(array((rows, CHI), jnp.bfloat16), array((rows // PHYS, CHI), jnp.float32)),
        in_specs=[SMEM] * 2 + [pl.BlockSpec(memory_space=pltpu.HBM)] * 9,
        out_specs=(VMEM,) * 2,
        scratch_shapes=[
            pltpu.VMEM((8 * SHARE, BLOCK), jnp.float32),
            pltpu.VMEM((CHI, CHI), jnp.float32),
            pltpu.VMEM((rows, CHI), jnp.float32),
            pltpu.VMEM((2, BLOCK, 2 * BLOCK), jnp.float32),
            pltpu.VMEM((2, BLOCK, 2 * BLOCK), jnp.float32),
            pltpu.SemaphoreType.DMA((9,)),
        ],
        compiler_params=settings(20),
        cost_estimate=cost(40 * 10**9, 8 * 10**6),
    )(index, place, *shares, target)


def shifted(block, axis, distance):
    count = lax.axis_size(axis)
    return lax.ppermute(block, axis, [((i - distance) % count, i) for i in range(count)])


def around(block, axis):
    return [block] + [shifted(block, axis, d) for d in (1, 2, 3)]


def scattered(blocks, axis):
    me = lax.axis_index(axis)
    out = []
    for d in range(4):
        block = lax.dynamic_index_in_dim(blocks, lax.rem(me + d, 4), 0, keepdims=False)
        out.append(shifted(block, axis, d) if d else block)
    return out


def summed(blocks):
    return (blocks[0] + blocks[1]) + (blocks[2] + blocks[3])


def shards(left_env, prev_left, cur_site, prev_site, hamiltonian, right_env, prev_right):
    own = left_env.shape[1]
    group = 4 * own
    left_own = jnp.transpose(left_env[0], (1, 0, 2)).reshape(MPOB * own, CHI)
    left_own = shifted(left_own, "seg", 1)
    x, y = lax.axis_index("bx"), lax.axis_index("by")
    place = jnp.stack([jnp.stack([lax.rem(i + 4 - d, 4) for d in range(4)]) for i in (x, y)])
    split = jnp.transpose(cur_site[0].reshape(own, PHYS, 4, group), (2, 0, 1, 3))
    split = jnp.stack(scattered(split.reshape(4, own, PHYS * group), "bx"))
    right = jnp.transpose(right_env[0], (1, 0, 2)).reshape(MPOB * own, CHI)
    ahead, behind = shifted(right, "by", 1), shifted(right, "by", 3)
    prev_now, right, left_own, split, ahead, behind = lax.optimization_barrier(
        (prev_left[0], right, left_own, split, ahead, behind)
    )
    right = [right, ahead, shifted(right, "by", 2), behind]
    prev_now = shifted(prev_now, "seg", 1)
    prev_now, hamiltonian = lax.optimization_barrier((prev_now, hamiltonian))
    same = jnp.eye(LANES, dtype=jnp.bfloat16)
    coupling = jnp.transpose(hamiltonian[0], (1, 2, 3, 0))
    coupling = coupling[:, None, :, :, :, None] * same[None, :, None, None, None, :]
    coupling = coupling.reshape(MPOB * LANES * PHYS, PHYS * MPOB * LANES)
    site = lax.all_gather(split, "by", axis=0)
    left = around(left_own, "bx")

    partial_value = jnp.einsum(
        "ab,bsc->asc", prev_now, prev_site[0], preferred_element_type=jnp.float32
    )
    partial_value = (-0.5 * partial_value).astype(jnp.bfloat16)
    partial_value = jnp.transpose(partial_value.reshape(4, 4, own * PHYS, own), (1, 0, 2, 3))
    partial_value, *_ = lax.optimization_barrier((partial_value, right[2], left[1], left[3]))
    partial_value = scattered(partial_value, "by")
    previous = lax.dynamic_slice_in_dim(prev_right[0], x * group, group, 0)

    mixed = mix(place, coupling, left, site)
    partial_value, mixed = lax.optimization_barrier((partial_value, mixed))
    shared = (place, right, previous, partial_value)
    sent = apply((2, 1, 3), *shared, (mixed[2], mixed[1], mixed[3]), jnp.bfloat16)
    (target,) = apply((0,), *shared, mixed[:1], jnp.float32)
    arrived = [shifted(v, "bx", -d) for v, d in zip(sent, (2, 1, 3))]
    target, *shares = correlate(place, target, arrived)

    halves = []
    for half, (axis, other) in enumerate((("bx", "by"), ("by", "bx"))):
        mine = shares[half * 4 : half * 4 + 4]
        mine = summed([mine[0]] + [shifted(mine[d], axis, d) for d in (1, 2, 3)])
        mine = summed(around(mine, other))
        halves += around(mine, axis)
    new_site, center = fit(lax.axis_index(BOND).reshape(1), place, halves, target)
    return (new_site.reshape(1, own, PHYS, CHI), center[None])


def solution(mesh):
    segments, bonds = mesh.devices.shape
    side = math.isqrt(bonds)
    grid = Mesh(mesh.devices.reshape(segments, side, side), ("seg", "bx", "by"))
    return jax.shard_map(
        shards,
        mesh=grid,
        in_specs=(
            P("seg", BOND, None, None),
            P("seg", None, None),
            P("seg", BOND, None, None),
            P("seg", None, None, BOND),
            P("seg", None, None, None, None),
            P("seg", BOND, None, None),
            P("seg", None, None),
        ),
        out_specs=(P("seg", BOND, None, None), P("seg", BOND, None)),
        check_vma=False,
    )
```
